256 devices in a mesh: fit: 4 (over x_lo, core), row: 64 (over y, x_hi, z).
Axes of the slice: x: 4 (x_hi: 2, x_lo: 2; x = x_hi * 2 + x_lo), y: 4, z: 8, core: 2. Of those that a mesh axis runs over, the one named last changes fastest.
Arguments:
- factors: bfloat16 [8192, 12, 512], P('row', 'fit'), may hold values from -2 to 2
Outputs:
- exchange: float32 [4, 8192, 2048], P('fit', 'row')
The draws below stay inside these ranges and needn't reach their ends.
All inputs are finite; a program needn't handle non-finite values.
Results may differ from the reference program's by a relative error of at most 0.0003.
Values may be sent and summed in bfloat16 or wider, within the bound.
No kernel may reach another device: no remote copies, remote signals or barrier semaphores. Data moves between devices by JAX's collectives and lax.ppermute only.
A program may use at most 128 MiB of HBM per device.

```python
import jax
import jax.numpy as jnp

NBF = 8192
NOCC = 512
NAUX = 12
ROWS = 128
N_FIT = 4
N_ROW = 64


def steps_of(stream_key, dims, shards, smallest, largest):
    def one(position, parts):
        heights = jax.random.uniform(jax.random.fold_in(jax.random.fold_in(stream_key, 6), position), (parts,), jnp.float32, smallest / len(shards), largest / len(shards))
        return jnp.repeat(jnp.exp(heights), dims[position] // parts).reshape((-1,) + (1,) * (len(dims) - position - 1))

    loudness = one(*shards[0])
    for cut in shards[1:]:
        loudness = loudness * one(*cut)
    return loudness


def gaussian(stream_key, dims, width, bound, shards=(), kind=jnp.bfloat16):
    result = jax.random.normal(stream_key, dims, jnp.float32) * width
    if len(shards) > 0:
        result = steps_of(stream_key, dims, shards, -0.22, 0.18) * result
    return jnp.clip(result, min=-bound, max=bound).astype(kind)


def setup_inputs(seed: int = 0) -> dict:
    arg_keys = jax.random.split(jax.random.key(seed), 2)
    return {
        "factors": gaussian(arg_keys[0], (NBF, NAUX, NOCC), 0.125, 2.0, ((0, 64), (1, 4))),
    }


def reference(factors):
    flat = factors.reshape(NBF, NAUX * NOCC)
    matrix = jnp.dot(flat, flat.T, preferred_element_type=jnp.float32)
    tiled = matrix.reshape(NBF, N_ROW, N_FIT, ROWS // N_FIT)
    return jnp.transpose(tiled, (2, 0, 1, 3)).reshape(N_FIT, NBF, NBF // N_FIT)
```

```python
import jax
import jax.numpy as jnp
from jax import lax
from jax.sharding import Mesh, PartitionSpec as P


def split_mesh(mesh):
    groups, rows = mesh.devices.shape
    cores, highs, lines = 2, 2, 8
    return Mesh(
        mesh.devices.reshape(groups // cores, cores, rows // (highs * lines), highs, lines),
        ("xl", "core", "y", "xh", "z"),
    )


def per_device(factors):
    rows, aux, occ = factors.shape
    local = factors.reshape(rows, aux * occ)
    groups = 4
    sub = rows // groups
    left = lax.all_gather(local, ("y", "xh"), axis=0, tiled=True)
    right = lax.all_gather(local, "z", axis=0, tiled=True)
    lines = lax.axis_size("z")
    planes = lax.axis_size(("y", "xh"))
    right = right.reshape(lines, groups, sub, aux * occ).transpose(1, 0, 2, 3).reshape(groups, lines * sub, aux * occ)
    product = lax.dot_general(
        right, left, (((2,), (1,)), ((), ())), preferred_element_type=jnp.float32
    )
    product = product.transpose(0, 2, 1)
    mine = lax.psum_scatter(product, ("xl", "core"), scatter_dimension=0, tiled=True)
    mine = mine.reshape(planes, rows, lines * sub)
    swapped = lax.all_to_all(mine, ("y", "xh"), split_axis=0, concat_axis=0, tiled=True)
    out = swapped.transpose(1, 0, 2).reshape(1, rows, planes * lines * sub)
    return out


def solution(mesh):
    return jax.shard_map(
        per_device,
        mesh=split_mesh(mesh),
        in_specs=(P(("y", "xh", "z"), ("xl", "core"), None),),
        out_specs=P(("xl", "core"), ("y", "xh", "z"), None),
        check_vma=False,
    )
```

```python
import functools

import jax
import jax.numpy as jnp
from jax import lax
from jax.experimental import pallas as pl
from jax.experimental.pallas import tpu as pltpu
from jax.sharding import Mesh, PartitionSpec as P

XL, CORE, Y, XH, Z = 2, 2, 4, 2, 8
AXES = ("xl", "core", "y", "xh", "z")


def split_mesh(mesh):
    return Mesh(mesh.devices.reshape(XL, CORE, Y, XH, Z), AXES)


def move(value, axes, target):
    sizes = {"xl": XL, "core": CORE, "y": Y, "xh": XH, "z": Z}
    dims = [sizes[a] for a in axes]
    count = 1
    for d in dims:
        count *= d
    pairs = []
    for source in range(count):
        rest, place = source, []
        for d in reversed(dims):
            place.insert(0, rest % d)
            rest //= d
        goal = target(*place)
        flat = 0
        for d, g in zip(dims, goal):
            flat = flat * d + g % d
        pairs.append((source, flat))
    return lax.ppermute(value, axes, pairs)


def turn(core, step):
    return step if core == 0 else -step


def along_z(value, step):
    return move(value, ("core", "z"), lambda c, z: (c, z + turn(c, step)))


def along_y(value, step):
    return move(value, ("core", "y"), lambda c, y: (c, y + turn(c, step)))


def across(value):
    return move(value, ("xh",), lambda h: (h + 1,))


def product_kernel(order, *refs):
    row_blocks, column_blocks = refs[:8], refs[8:16]
    send, keep, rows, columns, sems = refs[16:]
    aux, height, occ = row_blocks[0].shape
    copies = []
    for k in range(8):
        for a in range(aux):
            copies.append(
                pltpu.make_async_copy(
                    column_blocks[k].at[a],
                    columns.at[order[8 + k], :, pl.ds(a * occ, occ)],
                    sems.at[k * aux + a],
                )
            )
            copies.append(
                pltpu.make_async_copy(
                    row_blocks[k].at[a],
                    rows.at[order[k], :, pl.ds(a * occ, occ)],
                    sems.at[(8 + k) * aux + a],
                )
            )
    for c in copies:
        c.start()
    for c in copies:
        c.wait()
    sub = height // 4
    for slot in range(4):
        target = send if slot < 2 else keep
        first = pl.multiple_of(order[16 + slot] * sub, sub)
        picked = columns[:, pl.ds(first, sub), :].reshape(8 * sub, aux * occ)

        @pl.loop(0, 8)
        def _(k):
            target[slot % 2, k] = lax.dot_general(
                rows[k], picked, (((1,), (1,)), ((), ())), preferred_element_type=jnp.float32
            )


def products(order, row_blocks, column_blocks):
    aux, height, occ = row_blocks[0].shape
    shape = jax.ShapeDtypeStruct((2, 8, height, 2 * height), jnp.float32)
    return pl.pallas_call(
        product_kernel,
        out_shape=[shape, shape],
        in_specs=[pl.BlockSpec(memory_space=pltpu.SMEM)] + [pl.BlockSpec(memory_space=pl.ANY)] * 16,
        out_specs=[pl.BlockSpec(memory_space=pltpu.VMEM)] * 2,
        scratch_shapes=[
            pltpu.VMEM((8, height, aux * occ), jnp.bfloat16),
            pltpu.VMEM((8, height, aux * occ), jnp.bfloat16),
            pltpu.SemaphoreType.DMA((16 * aux,)),
        ],
        compiler_params=pltpu.CompilerParams(vmem_limit_bytes=32 * 1024 * 1024),
    )(order, *row_blocks, *column_blocks)


def assemble_kernel(order, *refs):
    out = refs[-1]
    for k in range(4):
        for h in range(2):
            first = pl.multiple_of(order[2 * k + h] * 256, 256)
            out[0, :, pl.ds(first, 256)] = refs[k][h]


def assemble(order, pieces):
    height = pieces[0].shape[1]
    return pl.pallas_call(
        assemble_kernel,
        out_shape=jax.ShapeDtypeStruct((1, height, 2048), jnp.float32),
        in_specs=[pl.BlockSpec(memory_space=pltpu.SMEM)] + [pl.BlockSpec(memory_space=pltpu.VMEM)] * 4,
        out_specs=pl.BlockSpec(memory_space=pltpu.VMEM),
    )(order, *pieces)


def per_device(factors):
    own = jnp.transpose(factors, (1, 0, 2))
    xl, core, y, xh, z = (lax.axis_index(a) for a in AXES)
    sign = 1 - 2 * core

    za1 = along_z(own, 1)
    zb1 = along_z(own, -1)
    ya1 = along_y(own, 1)
    yb1 = along_y(own, -1)
    x0 = across(own)
    za2 = along_z(za1, 1)
    zb2 = along_z(zb1, -1)
    ya2 = along_y(ya1, 1)
    xa1 = along_y(x0, 1)
    xb1 = along_y(x0, -1)
    za3 = along_z(za2, 1)
    zb3 = along_z(zb2, -1)
    xa2 = across(ya2)
    za4 = along_z(za3, 1)

    row_blocks = [own, ya1, yb1, ya2, x0, xa1, xb1, xa2]
    dy = [0, -sign, sign, 2]
    row_order = [dx * 4 + lax.rem(d + 4, 4) for dx in range(2) for d in dy]
    column_blocks = [own, za1, zb1, za2, zb2, za3, zb3, za4]
    dz = [0, -sign, sign, -2 * sign, 2 * sign, -3 * sign, 3 * sign, 4]
    column_order = [lax.rem(z + d + 8, 8) for d in dz]
    fit_order = [
        (1 - xl) * 2 + 1 - core,
        xl * 2 + 1 - core,
        (1 - xl) * 2 + core,
        xl * 2 + core,
    ]
    order = jnp.stack([jnp.int32(v) for v in row_order + column_order + fit_order])
    send, keep = products(order, row_blocks, column_blocks)
    summed = keep + move(send, ("core",), lambda c: (c + 1,))
    summed = summed.reshape(2, 2, 4, *summed.shape[2:])

    near = move(summed[0, 0], ("xl",), lambda a: (a + 1,))
    cross = move(summed[0, 1], ("xl", "xh"), lambda a, h: (a + 1, h + 1))
    far = across(summed[1, 1])
    t = jnp.stack([summed[1, 0] + near, cross + far], axis=1)
    pieces = [t[0]] + [move(t[d], ("y",), lambda b, d=d: (b + d,)) for d in range(1, 4)]
    places = [lax.rem(y - d + 4, 4) * 2 + lax.rem(xh + h, 2) for d in range(4) for h in range(2)]
    return assemble(jnp.stack(places).astype(jnp.int32), pieces)


def solution(mesh):
    return jax.shard_map(
        per_device,
        mesh=split_mesh(mesh),
        in_specs=(P(("y", "xh", "z"), ("xl", "core"), None),),
        out_specs=P(("xl", "core"), ("y", "xh", "z"), None),
        check_vma=False,
    )
```

```python
import functools

import jax
import jax.numpy as jnp
from jax import lax
from jax.experimental import pallas as pl
from jax.experimental.pallas import tpu as pltpu
from jax.sharding import Mesh, PartitionSpec as P

XL, CORE, Y, XH, Z = 2, 2, 4, 2, 8
AXES = ("xl", "core", "y", "xh", "z")


def split_mesh(mesh):
    return Mesh(mesh.devices.reshape(XL, CORE, Y, XH, Z), AXES)


def move(value, axes, target):
    sizes = {"xl": XL, "core": CORE, "y": Y, "xh": XH, "z": Z}
    dims = [sizes[a] for a in axes]
    count = 1
    for d in dims:
        count *= d
    pairs = []
    for source in range(count):
        rest, place = source, []
        for d in reversed(dims):
            place.insert(0, rest % d)
            rest //= d
        goal = target(*place)
        flat = 0
        for d, g in zip(dims, goal):
            flat = flat * d + g % d
        pairs.append((source, flat))
    return lax.ppermute(value, axes, pairs)


def along_z(value, step):
    return move(value, ("z",), lambda z: (z + step,))


def turn(core, step):
    return step if core == 0 else -step


def along_y(value, step):
    return move(value, ("core", "y"), lambda c, y: (c, y + turn(c, step)))


def across(value):
    return move(value, ("xh",), lambda h: (h + 1,))


def product_kernel(count, order, *refs):
    row_blocks, column_blocks = refs[:count], refs[count : count + 4]
    send, keep, rows, columns, row_sem, column_sem = refs[count + 4 :]
    aux, height, occ = row_blocks[0].shape
    sub = height // 4
    copies = []
    for k in range(4):
        for slot in range(4):
            copies.append(
                pltpu.make_async_copy(
                    column_blocks[k].at[:, pl.ds(pl.multiple_of(order[16 + slot] * sub, sub), sub), :],
                    columns.at[slot // 2, :, pl.ds(pl.multiple_of((slot % 2) * height + order[8 + k] * sub, sub), sub), :],
                    column_sem.at[k * 4 + slot],
                )
            )
    for k in range(count):
        place = pl.multiple_of(order[k] * height, height)
        copies.append(pltpu.make_async_copy(row_blocks[k], rows.at[:, pl.ds(place, height), :], row_sem.at[k]))
    for c in copies:
        c.start()
    for c in copies:
        c.wait()
    for half, target in enumerate((send, keep)):
        total = None
        for a in range(aux):
            part = lax.dot_general(
                rows[a], columns[half, a], (((1,), (1,)), ((), ())), preferred_element_type=jnp.float32
            )
            total = part if total is None else total + part
        for side in range(2):
            target[side] = total[:, side * height : (side + 1) * height]


def products(order, row_blocks, column_blocks):
    aux, height, occ = row_blocks[0].shape
    count = len(row_blocks)
    shape = jax.ShapeDtypeStruct((2, count * height, height), jnp.float32)
    return pl.pallas_call(
        functools.partial(product_kernel, count),
        out_shape=[shape, shape],
        in_specs=[pl.BlockSpec(memory_space=pltpu.SMEM)] + [pl.BlockSpec(memory_space=pl.ANY)] * (count + 4),
        out_specs=[pl.BlockSpec(memory_space=pltpu.VMEM)] * 2,
        scratch_shapes=[
            pltpu.VMEM((aux, count * height, occ), jnp.bfloat16),
            pltpu.VMEM((2, aux, 2 * height, occ), jnp.bfloat16),
            pltpu.SemaphoreType.DMA((count,)),
            pltpu.SemaphoreType.DMA((16,)),
        ],
        compiler_params=pltpu.CompilerParams(vmem_limit_bytes=32 * 1024 * 1024),
        cost_estimate=pl.CostEstimate(
            flops=2 * count * height * 4 * height * aux * occ, bytes_accessed=(count + 4) * aux * height * occ * 2, transcendentals=0
        ),
    )(order, *row_blocks, *column_blocks)


def assemble_kernel(order, *refs):
    out = refs[-1]
    height = out.shape[1]
    group = lax.broadcasted_iota(jnp.int32, (height, height), 1) // (height // 4)
    start = order[8]
    block = lax.rem(start + lax.rem(group - start + 8, 4), 8)
    low = block < 4
    for d in range(4):
        for h in range(2):
            first = pl.multiple_of(order[2 * d + h] * (2 * height), 2 * height)
            zero, one = refs[d][h], refs[4 + d][h]
            out[0, :, pl.ds(first, height)] = jnp.where(low, zero, one)
            out[0, :, pl.ds(first + height, height)] = jnp.where(low, one, zero)


def assemble(order, pieces):
    height = pieces[0].shape[1]
    return pl.pallas_call(
        assemble_kernel,
        out_shape=jax.ShapeDtypeStruct((1, height, 16 * height), jnp.float32),
        in_specs=[pl.BlockSpec(memory_space=pltpu.SMEM)] + [pl.BlockSpec(memory_space=pltpu.VMEM)] * 8,
        out_specs=pl.BlockSpec(memory_space=pltpu.VMEM),
    )(order, *pieces)


def swap_cores(send, keep):
    arrived = move(send, ("core",), lambda c: (c + 1,))
    return [keep[side] + arrived[side] for side in range(2)]


def split4(value):
    return value.reshape(4, value.shape[0] // 4, value.shape[1])


def per_device(factors):
    own = jnp.transpose(factors, (1, 0, 2))
    xl, core, y, xh, z = (lax.axis_index(a) for a in AXES)
    sign = 1 - 2 * core

    za1 = along_z(own, 1)
    zb1 = along_z(own, -1)
    ya1 = along_y(own, 1)
    yb1 = along_y(own, -1)
    x0 = across(own)
    za2 = along_z(za1, 1)
    zb2 = along_z(zb1, -1)
    ya2 = along_y(ya1, 1)
    xa1 = along_y(x0, 1)
    xb1 = along_y(x0, -1)
    za3 = along_z(za2, 1)
    zb3 = along_z(zb2, -1)
    xa2 = across(ya2)
    far_z = jnp.where(core == 0, za3, zb3)
    z4 = move(far_z, ("core", "z"), lambda c, k: (c, k + turn(c, 1)))

    dy = [0, -sign, sign, 2]
    row_order = [lax.rem(d + 4, 4) for d in dy]
    fit_order = [
        (1 - xl) * 2 + 1 - core,
        xl * 2 + 1 - core,
        (1 - xl) * 2 + core,
        xl * 2 + core,
    ]
    rows = [[own, ya1, yb1, ya2], [x0, xa1, xb1, xa2]]
    columns = [[own, za1, zb1, za2], [zb2, za3, zb3, z4]]
    shifts = [[0, -1, 1, -2], [2, -3, 3, 4]]

    def order(half):
        column_order = [lax.rem(z + d + 8, 4) for d in shifts[half]]
        values = row_order + [v + 4 for v in row_order] + column_order + [0] * 4 + fit_order
        return jnp.stack([jnp.int32(v) for v in values])

    sums = []
    for half in range(2):
        table = order(half)
        other0, mine0 = swap_cores(*products(table, rows[0], columns[half]))
        other1, mine1 = swap_cores(*products(table, rows[1], columns[half]))
        near = move(other0, ("xl",), lambda a: (a + 1,))
        cross = move(other1, ("xl", "xh"), lambda a, h: (a + 1, h + 1))
        far = across(mine1)
        sums.append(jnp.stack([split4(mine0 + near), split4(cross + far)], axis=1))

    pieces = []
    for half in range(2):
        t = sums[half]
        pieces += [t[0]] + [move(t[d], ("y",), lambda b, d=d: (b + d,)) for d in range(1, 4)]
    places = [lax.rem(y - d + 4, 4) * 2 + lax.rem(xh + h, 2) for d in range(4) for h in range(2)]
    places.append(lax.rem(z + 6, 8))
    return assemble(jnp.stack(places).astype(jnp.int32), pieces)


def solution(mesh):
    return jax.shard_map(
        per_device,
        mesh=split_mesh(mesh),
        in_specs=(P(("y", "xh", "z"), ("xl", "core"), None),),
        out_specs=P(("xl", "core"), ("y", "xh", "z"), None),
        check_vma=False,
    )
```

```python
import functools

import jax
import jax.numpy as jnp
from jax import lax
from jax.experimental import pallas as pl
from jax.experimental.pallas import tpu as pltpu
from jax.sharding import Mesh, PartitionSpec as P

XL, CORE, Y, XH, Z = 2, 2, 4, 2, 8
AXES = ("xl", "core", "y", "xh", "z")


def split_mesh(mesh):
    return Mesh(mesh.devices.reshape(XL, CORE, Y, XH, Z), AXES)


def move(value, axes, target):
    sizes = {"xl": XL, "core": CORE, "y": Y, "xh": XH, "z": Z}
    dims = [sizes[a] for a in axes]
    count = 1
    for d in dims:
        count *= d
    pairs = []
    for source in range(count):
        rest, place = source, []
        for d in reversed(dims):
            place.insert(0, rest % d)
            rest //= d
        goal = target(*place)
        flat = 0
        for d, g in zip(dims, goal):
            flat = flat * d + g % d
        pairs.append((source, flat))
    return lax.ppermute(value, axes, pairs)


def turn(core, step):
    return step if core == 0 else -step


def along_z(value, step):
    return move(value, ("core", "z"), lambda c, z: (c, z + turn(c, step)))


def along_y(value, step):
    return move(value, ("core", "y"), lambda c, y: (c, y + turn(c, step)))


def across(value):
    return move(value, ("xh",), lambda h: (h + 1,))


def product_kernel(slots, order, *refs):
    row_blocks, column_blocks = refs[:8], refs[8:16]
    targets = refs[-(len(slots) // 2) - 4 : -4]
    rows, columns, row_sem, column_sem = refs[-4:]
    aux, height, occ = row_blocks[0].shape
    sub = height // 4
    half_slots = len(slots) // 2
    column_copies, row_copies = [[] for _ in range(half_slots)], []
    for n, slot in enumerate(slots):
        for k in range(8):
            first = pl.multiple_of(order[16 + slot] * sub, sub)
            place = pl.multiple_of(n * 8 * sub + order[8 + k] * sub, sub)
            column_copies[n // 2].append(
                pltpu.make_async_copy(
                    column_blocks[k].at[:, pl.ds(first, sub), :],
                    columns.at[:, pl.ds(place, sub), :],
                    column_sem.at[k * len(slots) + n],
                )
            )
    for k in range(8):
        row_copies.append(
            pltpu.make_async_copy(row_blocks[k], rows.at[:, k * height : (k + 1) * height, :], row_sem.at[k])
        )
    for c in column_copies[0] + row_copies:
        c.start()
    for later in column_copies[1:]:
        for c in later:
            c.start()
    for n in range(half_slots):
        for c in column_copies[n]:
            c.wait()
        for t in range(0, 8, 2):
            if n == 0:
                for k in range(t, t + 2):
                    row_copies[k].wait()
            total = None
            for a in range(aux):
                part = lax.dot_general(
                    rows[a, t * height : (t + 2) * height],
                    columns[a, n * 16 * sub : (n + 1) * 16 * sub],
                    (((1,), (1,)), ((), ())),
                    preferred_element_type=jnp.float32,
                )
                total = part if total is None else total + part
            for k in range(t, t + 2):
                place = pl.multiple_of(order[k] * height, height)
                for side in range(2):
                    targets[n][side, pl.ds(place, height), :] = total[
                        (k - t) * height : (k - t + 1) * height, side * 8 * sub : (side + 1) * 8 * sub
                    ]


def products(order, row_blocks, column_blocks, slots, after=()):
    aux, height, occ = row_blocks[0].shape
    shape = jax.ShapeDtypeStruct((2, 8 * height, 2 * height), jnp.float32)
    return pl.pallas_call(
        functools.partial(product_kernel, slots),
        out_shape=[shape] * (len(slots) // 2),
        in_specs=[pl.BlockSpec(memory_space=pltpu.SMEM)] + [pl.BlockSpec(memory_space=pl.ANY)] * (16 + len(after)),
        out_specs=[pl.BlockSpec(memory_space=pltpu.VMEM)] * (len(slots) // 2),
        scratch_shapes=[
            pltpu.VMEM((aux, 8 * height, occ), jnp.bfloat16),
            pltpu.VMEM((aux, len(slots) * 2 * height, occ), jnp.bfloat16),
            pltpu.SemaphoreType.DMA((8,)),
            pltpu.SemaphoreType.DMA((8 * len(slots),)),
        ],
        compiler_params=pltpu.CompilerParams(vmem_limit_bytes=40 * 1024 * 1024),
    )(order, *row_blocks, *column_blocks, *after)


def assemble_kernel(got, out):
    step, height, width = got.shape[1:]
    for p in range(step):
        out[0, :, p * width : (p + 1) * width] = got[0, p] + got[1, p]


def assemble(got):
    count, height, width = got.shape[1:]
    step = 4
    return pl.pallas_call(
        assemble_kernel,
        grid=(count // step,),
        out_shape=jax.ShapeDtypeStruct((1, height, count * width), jnp.float32),
        in_specs=[pl.BlockSpec((2, step, height, width), lambda i: (0, i, 0, 0))],
        out_specs=pl.BlockSpec((1, height, step * width), lambda i: (0, 0, i)),
    )(got)


def per_device(factors):
    own = jnp.transpose(factors, (1, 0, 2))
    core, y, xh, z = (lax.axis_index(a) for a in AXES[1:])
    sign = 1 - 2 * core

    za1 = along_z(own, 1)
    zb1 = along_z(own, -1)
    ya1 = along_y(own, 1)
    yb1 = along_y(own, -1)
    x0 = across(own)
    za2 = along_z(za1, 1)
    zb2 = along_z(zb1, -1)
    ya2 = along_y(ya1, 1)
    xa1 = along_y(x0, 1)
    xb1 = along_y(x0, -1)
    za3 = along_z(za2, 1)
    zb3 = along_z(zb2, -1)
    xa2 = across(ya2)
    za4 = along_z(za3, 1)

    row_blocks = [own, ya1, yb1, ya2, x0, xa1, xb1, xa2]
    dy = [0, -sign, sign, 2]
    row_order = [lax.rem(y + d + 4, 4) * 2 + lax.rem(xh + dx, 2) for dx in range(2) for d in dy]
    column_blocks = [own, za1, zb1, za2, zb2, za3, zb3, za4]
    dz = [0, -sign, sign, -2 * sign, 2 * sign, -3 * sign, 3 * sign, 4]
    column_order = [lax.rem(z + d + 8, 8) for d in dz]
    fit_order = [1 - core, 3 - core, core, 2 + core]
    order = jnp.stack([jnp.int32(v) for v in row_order + column_order + fit_order])
    send, keep = products(order, row_blocks, column_blocks, (0, 1, 2, 3))
    summed = keep + move(send, ("core",), lambda c: (c + 1,))

    height, width = summed.shape[1] // 8, summed.shape[2]
    parts = summed.reshape(2 * 8, height, width)
    got = lax.all_to_all(parts, ("xl", "y", "xh"), split_axis=0, concat_axis=0, tiled=True)
    return assemble(got.reshape(2, 8, height, width))


def solution(mesh):
    return jax.shard_map(
        per_device,
        mesh=split_mesh(mesh),
        in_specs=(P(("y", "xh", "z"), ("xl", "core"), None),),
        out_specs=P(("xl", "core"), ("y", "xh", "z"), None),
        check_vma=False,
    )
```

```python
import functools

import jax
import jax.numpy as jnp
from jax import lax
from jax.experimental import pallas as pl
from jax.experimental.pallas import tpu as pltpu
from jax.sharding import Mesh, PartitionSpec as P

XL, CORE, Y, XH, Z = 2, 2, 4, 2, 8
AXES = ("xl", "core", "y", "xh", "z")


def split_mesh(mesh):
    return Mesh(mesh.devices.reshape(XL, CORE, Y, XH, Z), AXES)


def move(value, axes, target):
    sizes = {"xl": XL, "core": CORE, "y": Y, "xh": XH, "z": Z}
    dims = [sizes[a] for a in axes]
    count = 1
    for d in dims:
        count *= d
    pairs = []
    for source in range(count):
        rest, place = source, []
        for d in reversed(dims):
            place.insert(0, rest % d)
            rest //= d
        goal = target(*place)
        flat = 0
        for d, g in zip(dims, goal):
            flat = flat * d + g % d
        pairs.append((source, flat))
    return lax.ppermute(value, axes, pairs)


def turn(core, step):
    return step if core == 0 else -step


def along_z(value, step):
    return move(value, ("core", "z"), lambda c, z: (c, z + turn(c, step)))


def along_y(value, step):
    return move(value, ("core", "y"), lambda c, y: (c, y + turn(c, step)))


def across(value):
    return move(value, ("xh",), lambda h: (h + 1,))


def product_kernel(slots, order, *refs):
    row_blocks, column_blocks = refs[:8], refs[8:16]
    targets = refs[-(len(slots) // 2) - 4 : -4]
    rows, columns, row_sem, column_sem = refs[-4:]
    aux, height, occ = row_blocks[0].shape
    sub = height // 4
    half_slots = len(slots) // 2
    column_copies, row_copies = [[] for _ in range(half_slots)], []
    for n, slot in enumerate(slots):
        for k in range(8):
            first = pl.multiple_of(order[16 + slot] * sub, sub)
            place = pl.multiple_of(n * 8 * sub + order[8 + k] * sub, sub)
            column_copies[n // 2].append(
                pltpu.make_async_copy(
                    column_blocks[k].at[:, pl.ds(first, sub), :],
                    columns.at[:, pl.ds(place, sub), :],
                    column_sem.at[k * len(slots) + n],
                )
            )
    for k in range(8):
        row_copies.append(
            pltpu.make_async_copy(row_blocks[k], rows.at[:, k * height : (k + 1) * height, :], row_sem.at[k])
        )
    for c in column_copies[0] + row_copies:
        c.start()
    for later in column_copies[1:]:
        for c in later:
            c.start()
    for n in range(half_slots):
        for c in column_copies[n]:
            c.wait()
        for t in range(0, 8, 2):
            if n == 0:
                for k in range(t, t + 2):
                    row_copies[k].wait()
            total = None
            for a in range(aux):
                part = lax.dot_general(
                    rows[a, t * height : (t + 2) * height],
                    columns[a, n * 16 * sub : (n + 1) * 16 * sub],
                    (((1,), (1,)), ((), ())),
                    preferred_element_type=jnp.float32,
                )
                total = part if total is None else total + part
            for k in range(t, t + 2):
                place = pl.multiple_of(order[k] * height, height)
                for side in range(2):
                    targets[n][side, pl.ds(place, height), :] = total[
                        (k - t) * height : (k - t + 1) * height, side * 8 * sub : (side + 1) * 8 * sub
                    ]


def products(order, row_blocks, column_blocks, slots, after=()):
    aux, height, occ = row_blocks[0].shape
    shape = jax.ShapeDtypeStruct((2, 8 * height, 2 * height), jnp.float32)
    return pl.pallas_call(
        functools.partial(product_kernel, slots),
        out_shape=[shape] * (len(slots) // 2),
        in_specs=[pl.BlockSpec(memory_space=pltpu.SMEM)] + [pl.BlockSpec(memory_space=pl.ANY)] * (16 + len(after)),
        out_specs=[pl.BlockSpec(memory_space=pltpu.VMEM)] * (len(slots) // 2),
        scratch_shapes=[
            pltpu.VMEM((aux, 8 * height, occ), jnp.bfloat16),
            pltpu.VMEM((aux, len(slots) * 2 * height, occ), jnp.bfloat16),
            pltpu.SemaphoreType.DMA((8,)),
            pltpu.SemaphoreType.DMA((8 * len(slots),)),
        ],
        compiler_params=pltpu.CompilerParams(vmem_limit_bytes=16 * 1024 * 1024),
    )(order, *row_blocks, *column_blocks, *after)


def assemble_kernel(got, out):
    step, height, width = got.shape[1:]
    for p in range(step):
        out[0, :, p * width : (p + 1) * width] = got[0, p] + got[1, p]


def assemble(got):
    count, height, width = got.shape[1:]
    step = 4
    return pl.pallas_call(
        assemble_kernel,
        grid=(count // step,),
        out_shape=jax.ShapeDtypeStruct((1, height, count * width), jnp.float32),
        in_specs=[pl.BlockSpec((2, step, height, width), lambda i: (0, i, 0, 0))],
        out_specs=pl.BlockSpec((1, height, step * width), lambda i: (0, 0, i)),
    )(got)


def per_device(factors):
    own = jnp.transpose(factors, (1, 0, 2))
    core, y, xh, z = (lax.axis_index(a) for a in AXES[1:])
    sign = 1 - 2 * core

    za1 = along_z(own, 1)
    zb1 = along_z(own, -1)
    ya1 = along_y(own, 1)
    yb1 = along_y(own, -1)
    x0 = across(own)
    za2 = along_z(za1, 1)
    zb2 = along_z(zb1, -1)
    ya2 = along_y(ya1, 1)
    xa1 = along_y(x0, 1)
    xb1 = along_y(x0, -1)
    za3 = along_z(za2, 1)
    zb3 = along_z(zb2, -1)
    xa2 = across(ya2)
    za4 = along_z(za3, 1)

    row_blocks = [own, ya1, yb1, ya2, x0, xa1, xb1, xa2]
    dy = [0, -sign, sign, 2]
    row_order = [lax.rem(y + d + 4, 4) * 2 + lax.rem(xh + dx, 2) for dx in range(2) for d in dy]
    column_blocks = [own, za1, zb1, za2, zb2, za3, zb3, za4]
    dz = [0, -sign, sign, -2 * sign, 2 * sign, -3 * sign, 3 * sign, 4]
    column_order = [lax.rem(z + d + 8, 8) for d in dz]
    fit_order = [1 - core, 3 - core, core, 2 + core]
    order = jnp.stack([jnp.int32(v) for v in row_order + column_order + fit_order])
    (send,) = products(order, row_blocks, column_blocks, (0, 1))
    (keep,) = products(order, row_blocks, column_blocks, (2, 3), (send,))
    summed = keep + move(send, ("core",), lambda c: (c + 1,))

    height, width = summed.shape[1] // 8, summed.shape[2]
    parts = summed.reshape(2 * 8, height, width)
    got = lax.all_to_all(parts, ("xl", "y", "xh"), split_axis=0, concat_axis=0, tiled=True)
    return assemble(got.reshape(2, 8, height, width))


def solution(mesh):
    return jax.shard_map(
        per_device,
        mesh=split_mesh(mesh),
        in_specs=(P(("y", "xh", "z"), ("xl", "core"), None),),
        out_specs=P(("xl", "core"), ("y", "xh", "z"), None),
        check_vma=False,
    )
```

```python
import functools

import jax
import jax.numpy as jnp
from jax import lax
from jax.experimental import pallas as pl
from jax.experimental.pallas import tpu as pltpu
from jax.sharding import Mesh, PartitionSpec as P

XL, CORE, Y, XH, Z = 2, 2, 4, 2, 8
AXES = ("xl", "core", "y", "xh", "z")


def split_mesh(mesh):
    return Mesh(mesh.devices.reshape(XL, CORE, Y, XH, Z), AXES)


def move(value, axes, target):
    sizes = {"xl": XL, "core": CORE, "y": Y, "xh": XH, "z": Z}
    dims = [sizes[a] for a in axes]
    count = 1
    for d in dims:
        count *= d
    pairs = []
    for source in range(count):
        rest, place = source, []
        for d in reversed(dims):
            place.insert(0, rest % d)
            rest //= d
        goal = target(*place)
        flat = 0
        for d, g in zip(dims, goal):
            flat = flat * d + g % d
        pairs.append((source, flat))
    return lax.ppermute(value, axes, pairs)


def turn(core, step):
    return step if core == 0 else -step


def along_z(value, step):
    return move(value, ("core", "z"), lambda c, z: (c, z + turn(c, step)))


def along_y(value, step):
    return move(value, ("core", "y"), lambda c, y: (c, y + turn(c, step)))


def across(value):
    return move(value, ("xh",), lambda h: (h + 1,))


def product_kernel(slots, order, *refs):
    row_blocks, column_blocks = refs[:8], refs[8:16]
    targets = refs[-(len(slots) // 2) - 4 : -4]
    rows, columns, row_sem, column_sem = refs[-4:]
    aux, height, occ = row_blocks[0].shape
    sub = height // 4
    half_slots = len(slots) // 2
    column_copies, row_copies = [[] for _ in range(half_slots)], []
    for n, slot in enumerate(slots):
        for k in range(8):
            first = pl.multiple_of(order[16 + slot] * sub, sub)
            place = pl.multiple_of(n * 8 * sub + order[8 + k] * sub, sub)
            column_copies[n // 2].append(
                pltpu.make_async_copy(
                    column_blocks[k].at[:, pl.ds(first, sub), :],
                    columns.at[:, pl.ds(place, sub), :],
                    column_sem.at[k * len(slots) + n],
                )
            )
    for k in range(8):
        row_copies.append(
            pltpu.make_async_copy(row_blocks[k], rows.at[:, k * height : (k + 1) * height, :], row_sem.at[k])
        )
    for c in column_copies[0] + row_copies:
        c.start()
    for later in column_copies[1:]:
        for c in later:
            c.start()
    for n in range(half_slots):
        for c in column_copies[n]:
            c.wait()
        for t in range(0, 8, 4):
            if n == 0:
                for k in range(t, t + 4):
                    row_copies[k].wait()
            total = None
            for a in range(aux):
                part = lax.dot_general(
                    rows[a, t * height : (t + 4) * height],
                    columns[a, n * 16 * sub : (n + 1) * 16 * sub],
                    (((1,), (1,)), ((), ())),
                    preferred_element_type=jnp.float32,
                )
                total = part if total is None else total + part
            for k in range(t, t + 4):
                place = pl.multiple_of(order[k] * height, height)
                for side in range(2):
                    targets[n][side, pl.ds(place, height), :] = total[
                        (k - t) * height : (k - t + 1) * height, side * 8 * sub : (side + 1) * 8 * sub
                    ]


def products(order, row_blocks, column_blocks, slots, after=()):
    aux, height, occ = row_blocks[0].shape
    shape = jax.ShapeDtypeStruct((2, 8 * height, 2 * height), jnp.float32)
    return pl.pallas_call(
        functools.partial(product_kernel, slots),
        out_shape=[shape] * (len(slots) // 2),
        in_specs=[pl.BlockSpec(memory_space=pltpu.SMEM)] + [pl.BlockSpec(memory_space=pl.ANY)] * (16 + len(after)),
        out_specs=[pl.BlockSpec(memory_space=pltpu.VMEM)] * (len(slots) // 2),
        scratch_shapes=[
            pltpu.VMEM((aux, 8 * height, occ), jnp.bfloat16),
            pltpu.VMEM((aux, len(slots) * 2 * height, occ), jnp.bfloat16),
            pltpu.SemaphoreType.DMA((8,)),
            pltpu.SemaphoreType.DMA((8 * len(slots),)),
        ],
        compiler_params=pltpu.CompilerParams(vmem_limit_bytes=16 * 1024 * 1024),
    )(order, *row_blocks, *column_blocks, *after)


def assemble_kernel(got, out):
    step, height, width = got.shape[1:]
    for p in range(step):
        out[0, :, p * width : (p + 1) * width] = got[0, p] + got[1, p]


def assemble(got):
    count, height, width = got.shape[1:]
    step = 4
    return pl.pallas_call(
        assemble_kernel,
        grid=(count // step,),
        out_shape=jax.ShapeDtypeStruct((1, height, count * width), jnp.float32),
        in_specs=[pl.BlockSpec((2, step, height, width), lambda i: (0, i, 0, 0))],
        out_specs=pl.BlockSpec((1, height, step * width), lambda i: (0, 0, i)),
    )(got)


def per_device(factors):
    own = jnp.transpose(factors, (1, 0, 2))
    core, y, xh, z = (lax.axis_index(a) for a in AXES[1:])
    sign = 1 - 2 * core

    za1 = along_z(own, 1)
    zb1 = along_z(own, -1)
    ya1 = along_y(own, 1)
    yb1 = along_y(own, -1)
    x0 = across(own)
    za2 = along_z(za1, 1)
    zb2 = along_z(zb1, -1)
    ya2 = along_y(ya1, 1)
    xa1 = along_y(x0, 1)
    xb1 = along_y(x0, -1)
    za3 = along_z(za2, 1)
    zb3 = along_z(zb2, -1)
    xa2 = across(ya2)
    za4 = along_z(za3, 1)

    row_blocks = [own, ya1, yb1, ya2, x0, xa1, xb1, xa2]
    dy = [0, -sign, sign, 2]
    row_order = [lax.rem(y + d + 4, 4) * 2 + lax.rem(xh + dx, 2) for dx in range(2) for d in dy]
    column_blocks = [own, za1, zb1, za2, zb2, za3, zb3, za4]
    dz = [0, -sign, sign, -2 * sign, 2 * sign, -3 * sign, 3 * sign, 4]
    column_order = [lax.rem(z + d + 8, 8) for d in dz]
    fit_order = [1 - core, 3 - core, core, 2 + core]
    order = jnp.stack([jnp.int32(v) for v in row_order + column_order + fit_order])
    (send,) = products(order, row_blocks, column_blocks, (0, 1))
    (keep,) = products(order, row_blocks, column_blocks, (2, 3), (send,))
    summed = keep + move(send, ("core",), lambda c: (c + 1,))

    height, width = summed.shape[1] // 8, summed.shape[2]
    parts = summed.reshape(2 * 8, height, width)
    got = lax.all_to_all(parts, ("xl", "y", "xh"), split_axis=0, concat_axis=0, tiled=True)
    return assemble(got.reshape(2, 8, height, width))


def solution(mesh):
    return jax.shard_map(
        per_device,
        mesh=split_mesh(mesh),
        in_specs=(P(("y", "xh", "z"), ("xl", "core"), None),),
        out_specs=P(("xl", "core"), ("y", "xh", "z"), None),
        check_vma=False,
    )
```
